256 devices in a mesh: pair: 64 (over y, x_hi, z), aux: 4 (over x_lo, core).
Axes of the slice: x: 4 (x_hi: 2, x_lo: 2; x = x_hi * 2 + x_lo), y: 4, z: 8, core: 2. Of those that a mesh axis runs over, the one named last changes fastest.
Arguments:
- x_panels: float32 [1024, 8192], P(None, 'pair'), may hold values from -0.1875 to 0.1875
- xbar_panels: float32 [1024, 8192], P(None, 'pair'), may hold values from -6 to 6
- bbar_below: float32 [4096, 8192], P('aux', 'pair'), may hold values from -16 to 16
- l_below: float32 [4096, 1024], P(('aux', 'pair')), may hold values from -0.09375 to 0.09375
- l_cross: float32 [512, 512], P('pair'), may hold values from -0.25 to 0.25
- dinv: float32 [2, 512, 512], P(None, 'pair'), as said below
Outputs:
- bbar_panels: float32 [1024, 8192], P(None, 'pair')
- lbar_below: float32 [4096, 1024], P(('aux', 'pair'))
- lbar_diag: float32 [2, 512, 512], P(None, 'pair')
- lbar_cross: float32 [512, 512], P('pair')
The draws below stay inside these ranges and needn't reach their ends.
Inputs may be any that keep to these rules, and one draw needn't show every extreme that they name: Each dinv[k] is lower triangular with a positive diagonal.
All inputs are finite; a program needn't handle non-finite values.
Results may differ from the reference program's by a relative error of at most 0.00013.
Values sent between devices are 32-bit elements; how exact they have to be, the bound alone decides.
A program may use at most 64 MiB of HBM per device.

```python
import jax
import jax.numpy as jnp
from jax import lax

NB = 512
PAIRS = 8192
ROWS = 4096


def draw_dinv(key, part):
    first_key, second_key = jax.random.split(jax.random.fold_in(key, 7))
    rows_idx = jnp.arange(NB)[:, None]
    cols_idx = jnp.arange(NB)[None, :]
    lower_mask = (rows_idx > cols_idx).astype(jnp.float32)
    diag_vals = jax.random.uniform(first_key, (2, NB), jnp.float32, 0.5, 2.0)
    spread = 1.0
    lower_vals = jax.random.normal(second_key, (2, NB, NB), jnp.float32) * (spread / jnp.sqrt(1.0 * NB))
    eye_mat = (rows_idx == cols_idx).astype(jnp.float32)
    return lower_vals * lower_mask[None] + diag_vals[:, :, None] * eye_mat[None]


def strengthened(result, key, source, target, parts, factor):
    owner, partner = [(jnp.arange(result.shape[axis_at]) // (result.shape[axis_at] // parts)).reshape([-1 if axis == axis_at else 1 for axis in range(result.ndim)]) for axis_at in (source, target)]
    chosen = jax.random.permutation(key, parts)[partner]
    strong = (owner == chosen) | (owner == (partner + parts // 2) % parts)
    return jnp.where(strong, factor * result, result)


def block_levels(key, dims, cuts, smallest, high):
    def one(axis_at, shards_of):
        heights = jax.random.uniform(jax.random.fold_in(jax.random.fold_in(key, 6), axis_at), (shards_of,), jnp.float32, smallest / len(cuts), high / len(cuts))
        return jnp.repeat(jnp.exp(heights), dims[axis_at] // shards_of).reshape((-1,) + (1,) * (len(dims) - axis_at - 1))

    gain = one(*cuts[0])
    for cut in cuts[1:]:
        gain = gain * one(*cut)
    return gain


def normal_values(rng, dims, scale, most, cuts=(), dtype=jnp.bfloat16):
    factor_of = block_levels(rng, dims, cuts, -0.22, 0.18) if cuts else 1.0
    entries = jax.random.normal(rng, dims, jnp.float32) * scale * factor_of
    return jnp.minimum(jnp.maximum(entries, -most), most).astype(dtype)


def noise_with(own_key, dims, scale, most, cuts, heavy, held_as=jnp.bfloat16):
    entries = scale * jax.random.normal(own_key, dims, jnp.float32)
    if cuts:
        entries = entries * block_levels(own_key, dims, cuts, -0.22, 0.18)
    return jnp.clip(strengthened(entries, jax.random.fold_in(own_key, 3), *heavy), -most, most).astype(held_as)


def setup_inputs(seed: int = 0) -> dict:
    keys = jax.random.split(jax.random.key(seed), 7)
    x_panels = noise_with(keys[0], (2 * NB, PAIRS), PAIRS ** -0.5, 0.1875, ((1, 64),), (1, 0, 64, 4.0), jnp.float32)
    xbar_panels = normal_values(keys[1], (2 * NB, PAIRS), 1.0, 6.0, ((1, 64),), jnp.float32)
    bbar_below = noise_with(keys[2], (ROWS, PAIRS), 1.0, 16.0, ((0, 4), (1, 64)), (1, 0, 64, 4.0), jnp.float32)
    l_below = normal_values(keys[3], (ROWS, 2 * NB), ROWS ** -0.5, 0.09375, ((0, 256),), jnp.float32)
    l_cross = normal_values(keys[4], (NB, NB), NB ** -0.5, 0.25, ((0, 64),), jnp.float32)
    dinv = draw_dinv(jax.random.fold_in(keys[6], 71), 0)
    return {"x_panels": x_panels, "xbar_panels": xbar_panels, "bbar_below": bbar_below, "l_below": l_below, "l_cross": l_cross, "dinv": dinv}


def reference(x_panels, xbar_panels, bbar_below, l_below, l_cross, dinv):
    precise = lax.Precision.HIGHEST
    corr = jnp.dot(l_below.T, bbar_below, precision=precise, preferred_element_type=jnp.float32)
    lbar_below = -jnp.dot(bbar_below, x_panels.T, precision=precise, preferred_element_type=jnp.float32)
    bbar_late = jnp.dot(dinv[1].T, xbar_panels[NB:] - corr[NB:], precision=precise, preferred_element_type=jnp.float32)
    cross_term = jnp.dot(l_cross.T, bbar_late, precision=precise, preferred_element_type=jnp.float32)
    bbar_early = jnp.dot(dinv[0].T, xbar_panels[:NB] - corr[:NB] - cross_term, precision=precise, preferred_element_type=jnp.float32)
    x_early = x_panels[:NB]
    x_late = x_panels[NB:]
    diag_early = -jnp.dot(bbar_early, x_early.T, precision=precise, preferred_element_type=jnp.float32)
    diag_late = -jnp.dot(bbar_late, x_late.T, precision=precise, preferred_element_type=jnp.float32)
    lbar_cross = -jnp.dot(bbar_late, x_early.T, precision=precise, preferred_element_type=jnp.float32)
    bbar_panels = jnp.concatenate([bbar_early, bbar_late], axis=0)
    return bbar_panels, lbar_below, jnp.stack([diag_early, diag_late]), lbar_cross
```

```python
import jax
import jax.numpy as jnp
from jax import lax
from jax.experimental import pallas as pl
from jax.experimental.pallas import tpu as pltpu
from jax.sharding import PartitionSpec as P

MESH = pl.DeviceIdType.MESH
F32 = jnp.float32
BF16 = jnp.bfloat16
NN = ((1,), (0,))
NT = ((1,), (1,))

L_Z, L_H, B_Y, G_Z, G_Y, G_H, X_Y, X_C = 0, 8, 16, 20, 28, 32, 36, 40
R_C, R_Y, R_L, S_C, D_Y, C_Y, D_H, D_Z, D_A, F_Z, F_H = (
    44, 46, 54, 56, 60, 64, 68, 70, 78, 82, 90)
COPIES = 92

Z_ORDER = (1, 7, 2, 6, 3, 5, 4)


def halves(value):
    high = value.astype(BF16)
    return high, (value - high.astype(F32)).astype(BF16)


def dot3(a, b, dims):
    def one(s, t):
        return lax.dot_general(s, t, (dims, ((), ())), preferred_element_type=F32)

    return one(a[0], b[0]) + (one(a[0], b[1]) + one(a[1], b[0]))


def kernel(
    x_ref, xbar_ref, bbar_ref, l_ref, lc_ref, dinv_ref,
    panels_ref, lbelow_ref, ldiag_ref, lcross_ref,
    lg, lh, ll, gs, gh, gl, bb, bh, bl, th, tl, xx, xh, xl, xbt,
    cks, csend, crv, yr, accs, accr, lt, et, ch,
    dd, ddr, dc, dcr, ds, dhr, ez, ezr, fin, pp, zr, ps, hr,
    ss, rs,
):
    pair = lax.axis_index("pair")
    aux = lax.axis_index("aux")
    y, h, z = pair // 16, (pair // 8) % 2, pair % 8
    lo, core = aux // 2, aux % 2

    def at(dy=0, dh=0, dz=0, dl=0, dcore=0):
        place = ((y + dy) % 4 * 2 + (h + dh) % 2) * 8 + (z + dz) % 8
        return (place, (lo + dl) % 2 * 2 + (core + dcore) % 2)

    started = []

    def send(src, dst, place, to):
        copy = pltpu.make_async_remote_copy(
            src_ref=src, dst_ref=dst, send_sem=ss.at[place], recv_sem=rs.at[place],
            device_id=to, device_id_type=MESH)
        copy.start()
        return copy

    def keep(src, dst, place, to):
        copy = send(src, dst, place, to)
        started.append(copy)
        return copy

    lg[h, z] = l_ref[...]
    gs[y, h, z, :, 0:512] = jnp.where(core == 0, dinv_ref[0], dinv_ref[1])
    gs[y, h, z, :, 512:768] = jnp.where(core == 0, lc_ref[:, 0:256], lc_ref[:, 256:512])

    barrier = pltpu.get_barrier_semaphore()
    partners = [at(dy=d) for d in (1, 2, 3)] + [at(dz=k) for k in range(1, 8)]
    partners += [at(dh=1), at(dl=1), at(dcore=1), at(dl=1, dcore=1)]
    for partner in partners:
        pl.semaphore_signal(barrier, inc=1, device_id=partner, device_id_type=MESH)
    pl.semaphore_wait(barrier, len(partners))

    mine = lg.at[h, z]
    l_z = {k: keep(mine, mine, L_Z + k, at(dz=k)) for k in Z_ORDER}
    l_h = {0: keep(mine, mine, L_H, at(dh=1))}
    b_y = {}
    for d in (2, 1, 3):
        rows = pl.ds((y + d) % 4 * 256, 256)
        b_y[d] = keep(bbar_ref.at[rows], bb.at[d - 1], B_Y + d, at(dy=d))
    mine = gs.at[y, h, z]
    g_z = {k: keep(mine, mine, G_Z + k, at(dz=k)) for k in Z_ORDER}

    def take_b(d, value):
        cols = slice(d * 128, (d + 1) * 128)
        high, low = halves(value)
        bh[:, cols] = high
        bl[:, cols] = low
        high, low = halves(value.T)
        th[cols, :] = high
        tl[cols, :] = low

    take_b(0, bbar_ref[pl.ds(y * 256, 256), :])

    def l_forward(k):
        l_z[k].wait_recv()
        block = lg.at[h, (z + 8 - k) % 8]
        l_h[k] = keep(block, block, L_H + k, at(dh=1))

    l_forward(1)
    l_forward(7)
    xbt[...] = xbar_ref[pl.ds(core * 512, 512), :].T
    l_forward(2)
    l_forward(6)
    for d in (1, 3):
        b_y[d].wait_recv()
        take_b(d, bb[d - 1])
    l_forward(3)
    l_forward(5)
    l_forward(4)
    b_y[2].wait_recv()
    take_b(2, bb[1])

    for k in Z_ORDER:
        g_z[k].wait_recv()
    mine = gs.at[y, h]
    g_y = {d: keep(mine, mine, G_Y + d, at(dy=d)) for d in (1, 3, 2)}
    g_h = {0: keep(mine, mine, G_H, at(dh=1))}

    half = x_ref.at[pl.ds(core * 512, 512)]
    x_y = {d: keep(half, xx.at[d - 1, core], X_Y + d, at(dy=d)) for d in (1, 3, 2)}
    high, low = halves(x_ref[...])
    xh[:, 0:128] = high
    xl[:, 0:128] = low

    for k in (0,) + Z_ORDER:
        l_h[k].wait_recv()
    for part in range(2):
        high, low = halves(lg[:, :, :, part * 512 : (part + 1) * 512].reshape(256, 512))
        lh[part] = high
        ll[part] = low

    turned = (th[...], tl[...])
    r_c = []
    for q in range(2):
        cols = slice(q * 256, (q + 1) * 256)
        other = (lh[1 - core, :, cols], ll[1 - core, :, cols])
        csend[q] = dot3(turned, other, NN).reshape(4, 128, 256)
        r_c.append(keep(csend.at[q], crv.at[q], R_C + q, at(dcore=1)))
        own = (lh[core, :, cols], ll[core, :, cols])
        cks[q] = dot3(turned, own, NN).reshape(4, 128, 256)
    r_y = {}
    for q in range(2):
        r_c[q].wait_recv()
        for d in (2, 1, 3, 0):
            cks[q, d] += crv[q, d]
            if d:
                r_y[q, d] = keep(cks.at[q, d], yr.at[q, d - 1], R_Y + 4 * q + d, at(dy=4 - d))

    for d in (1, 3, 2):
        g_y[d].wait_recv()
        block = gs.at[(y + 4 - d) % 4, h]
        g_h[d] = keep(block, block, G_H + d, at(dh=1))

    r_l = []
    for q in range(2):
        for d in (1, 3, 2):
            r_y[q, d].wait_recv()
        accs[q] = (cks[q, 0] + yr[q, 0]) + (yr[q, 1] + yr[q, 2])
        r_l.append(keep(accs.at[q], accr.at[q], R_L + q, at(dl=1)))

    x_c = {}
    for d in (1, 3, 2):
        x_y[d].wait_recv()
        block = xx.at[d - 1, core]
        x_c[d] = keep(block, block, X_C + d, at(dcore=1))
    for d in (1, 3, 2):
        x_c[d].wait_recv()
        cols = slice(d * 128, (d + 1) * 128)
        high, low = halves(xx[d - 1].reshape(1024, 128))
        xh[:, cols] = high
        xl[:, cols] = low
    for part in range(4):
        rows = slice(part * 256, (part + 1) * 256)
        product = dot3((bh[...], bl[...]), (xh[rows, :], xl[rows, :]), NT)
        pp[:, :, :, rows] = product.reshape(2, 8, 16, 256)
    f_z = {k: keep(pp.at[:, (z + k) % 8], zr.at[k - 1], F_Z + k, at(dz=k)) for k in Z_ORDER}

    for d in (0, 1, 3, 2):
        g_h[d].wait_recv()
    high, low = halves(gs[...].reshape(512, 768))
    gh[...] = high
    gl[...] = low
    for q in range(2):
        r_l[q].wait_recv()

    def x_rows(start, count):
        rows = pl.ds(pl.multiple_of(start, 128), count)
        return xh[rows, 0:128], xl[rows, 0:128]

    def block_of(columns):
        return gh[:, columns], gl[:, columns]

    solve_cols, cross_cols = slice(0, 512), slice(512, 768)
    to_core = at(dcore=1)

    def copy_of(ref, place):
        return pltpu.make_async_remote_copy(
            src_ref=ref, dst_ref=ref, send_sem=ss.at[place], recv_sem=rs.at[place],
            device_id=to_core, device_id_type=MESH)

    def corrected():
        return xbt[...] - jnp.concatenate([accs[0] + accr[0], accs[1] + accr[1]], axis=1)

    def diag_product(turned_rows):
        rows = turned_rows.T
        product = dot3(halves(rows), x_rows(core * 512 + lo * 256, 256), NT)
        dd[...] = product.reshape(4, 128, 256)
        return rows

    @pl.when(core == 1)
    def _():
        late = dot3(halves(corrected()), block_of(solve_cols), NN)
        lt[...] = late
        copy_of(lt, S_C).start()
        ch[...] = dot3(halves(late), block_of(cross_cols), NN)
        copy_of(ch, S_C + 1).start()
        panels_ref[512:1024, :] = diag_product(late)

    @pl.when(core == 0)
    def _():
        rest = corrected()
        copy_of(lt, S_C).wait_recv()
        cross = dot3(halves(lt[...]), block_of(cross_cols), NN)
        copy_of(ch, S_C + 1).wait_recv()
        rest = rest - jnp.concatenate([cross, ch[...]], axis=1)
        early = dot3(halves(rest), block_of(solve_cols), NN)
        et[...] = early
        copy_of(et, S_C + 2).start()
        panels_ref[0:512, :] = diag_product(early)

    d_y = {}
    for d in (2, 1, 3):
        d_y[d] = keep(dd.at[(y + d) % 4], ddr.at[d - 1], D_Y + d, at(dy=d))
    late = lt[...].T
    product = dot3(halves(late), x_rows(aux * 128, 128), NT)
    dc[...] = product.reshape(4, 128, 128)
    c_y = {}
    for d in (2, 1, 3):
        c_y[d] = keep(dc.at[(y + d) % 4], dcr.at[d - 1], C_Y + d, at(dy=d))

    @pl.when(core == 0)
    def _():
        panels_ref[512:1024, :] = late

    for k in Z_ORDER:
        f_z[k].wait_recv()
    total = pp[:, z]
    for k in range(7):
        total = total + zr[k]
    ps[...] = total
    f_h = keep(ps.at[1 - h], hr, F_H, at(dh=1))

    for d in (1, 3, 2):
        d_y[d].wait_recv()
        c_y[d].wait_recv()
    total = (dd[y] + ddr[0]) + (ddr[1] + ddr[2])
    ds[:, :, :, 0:256] = total.reshape(2, 8, 8, 256)
    total = (dc[y] + dcr[0]) + (dcr[1] + dcr[2])
    ds[:, :, :, 256:384] = total.reshape(2, 8, 8, 128)
    d_h = keep(ds.at[1 - h], dhr, D_H, at(dh=1))

    f_h.wait_recv()
    lbelow_ref[...] = -(ps[h] + hr[...])

    @pl.when(core == 1)
    def _():
        copy_of(et, S_C + 2).wait_recv()
        panels_ref[0:512, :] = et[...].T
        copy_of(lt, S_C).wait_send()
        copy_of(ch, S_C + 1).wait_send()

    @pl.when(core == 0)
    def _():
        copy_of(et, S_C + 2).wait_send()

    d_h.wait_recv()
    ez[...] = ds[h] + dhr[...]
    d_z = {k: keep(ez.at[(z + k) % 8], ezr.at[k - 1], D_Z + k, at(dz=k)) for k in Z_ORDER}
    for k in Z_ORDER:
        d_z[k].wait_recv()
    total = ez[z]
    for k in range(7):
        total = total + ezr[k]
    fin[aux] = -total
    d_a = []
    for j in (1, 2, 3):
        block = fin.at[aux]
        d_a.append(keep(block, block, D_A + j, at(dl=j // 2, dcore=j % 2)))
    for copy in d_a:
        copy.wait_recv()
    for part in range(4):
        which, side = part % 2, part // 2
        ldiag_ref[which, :, side * 256 : (side + 1) * 256] = fin[part, :, 0:256]
        lcross_ref[:, part * 128 : (part + 1) * 128] = fin[part, :, 256:384]

    for copy in started:
        copy.wait_send()


def body(x_panels, xbar_panels, bbar_below, l_below, l_cross, dinv):
    def vmem(*shape, dtype=F32):
        return pltpu.VMEM(shape, dtype)

    outs = (
        jax.ShapeDtypeStruct((1024, 128), F32),
        jax.ShapeDtypeStruct((16, 1024), F32),
        jax.ShapeDtypeStruct((2, 8, 512), F32),
        jax.ShapeDtypeStruct((8, 512), F32),
    )
    scratch = [
        vmem(2, 8, 16, 1024),
        vmem(2, 256, 512, dtype=BF16), vmem(2, 256, 512, dtype=BF16),
        vmem(4, 2, 8, 8, 768),
        vmem(512, 768, dtype=BF16), vmem(512, 768, dtype=BF16),
        vmem(3, 256, 128),
        vmem(256, 512, dtype=BF16), vmem(256, 512, dtype=BF16),
        vmem(512, 256, dtype=BF16), vmem(512, 256, dtype=BF16),
        vmem(3, 2, 512, 128),
        vmem(1024, 512, dtype=BF16), vmem(1024, 512, dtype=BF16),
        vmem(128, 512),
        vmem(2, 4, 128, 256), vmem(2, 4, 128, 256), vmem(2, 4, 128, 256),
        vmem(2, 3, 128, 256),
        vmem(2, 128, 256), vmem(2, 128, 256),
        vmem(128, 512), vmem(128, 512), vmem(128, 256),
        vmem(4, 128, 256), vmem(3, 128, 256),
        vmem(4, 128, 128), vmem(3, 128, 128),
        vmem(2, 8, 8, 384), vmem(8, 8, 384),
        vmem(8, 8, 384), vmem(7, 8, 384), vmem(4, 8, 384),
        vmem(2, 8, 16, 1024), vmem(7, 2, 16, 1024),
        vmem(2, 16, 1024), vmem(16, 1024),
        pltpu.SemaphoreType.DMA((COPIES,)), pltpu.SemaphoreType.DMA((COPIES,)),
    ]
    return pl.pallas_call(
        kernel,
        out_shape=outs,
        in_specs=[pl.BlockSpec(memory_space=pltpu.VMEM)] * 6,
        out_specs=(pl.BlockSpec(memory_space=pltpu.VMEM),) * 4,
        scratch_shapes=scratch,
        compiler_params=pltpu.CompilerParams(
            collective_id=0, has_side_effects=True, vmem_limit_bytes=50 * 1024 * 1024),
        name="panel_steps",
    )(x_panels, xbar_panels, bbar_below, l_below, l_cross, dinv)


def solution(mesh):
    in_specs = (
        P(None, "pair"),
        P(None, "pair"),
        P("aux", "pair"),
        P(("aux", "pair"), None),
        P("pair", None),
        P(None, "pair", None),
    )
    out_specs = (P(None, "pair"), P(("aux", "pair"), None), P(None, "pair", None), P("pair", None))
    return jax.shard_map(body, mesh=mesh, in_specs=in_specs, out_specs=out_specs, check_vma=False)
```

```python
import jax
import jax.numpy as jnp
from jax import lax
from jax.experimental import pallas as pl
from jax.experimental.pallas import tpu as pltpu
from jax.sharding import PartitionSpec as P

MESH = pl.DeviceIdType.MESH
F32 = jnp.float32
BF16 = jnp.bfloat16
NN = ((1,), (0,))
NT = ((1,), (1,))

CHUNKS = 2
WIDE = 512 // CHUNKS
COPIES = 160
LOADS = 6

Z_ORDER = (1, 7, 2, 6, 3, 5, 4)

STARTS = (0, 384, 896, 1536)
PACKED = 2304


def halves(value):
    high = value.astype(BF16)
    return high, (value - high.astype(F32)).astype(BF16)


def dot3(a, b, dims):
    def one(s, t):
        return lax.dot_general(s, t, (dims, ((), ())), preferred_element_type=F32)

    return one(a[0], b[0]) + (one(a[0], b[1]) + one(a[1], b[0]))


def kernel(
    x_ref, xbar_ref, bbar_ref, l_ref, lc_ref, dinv_ref,
    panels_ref, lbelow_ref, ldiag_ref, lcross_ref,
    x_in, xbar_in, b_in, l_in, lc_in, dinv_in,
    lg, lh, ll, gy, gs, gh, gl, bb, bh, bl, th, tl, xx, xh, xl, xbt,
    cks, csend, crv, yr, accs, accr, pt, ot, ch, ta,
    ds, er, fin, pp, zr, ps, hr,
    ss, rs, ls,
):
    pair = lax.axis_index("pair")
    aux = lax.axis_index("aux")
    y, h, z = pair // 16, (pair // 8) % 2, pair % 8
    lo, core = aux // 2, aux % 2

    def at(dy=0, dh=0, dz=0, dl=0, dcore=0):
        place = ((y + dy) % 4 * 2 + (h + dh) % 2) * 8 + (z + dz) % 8
        return (place, (lo + dl) % 2 * 2 + (core + dcore) % 2)

    started = []
    places = iter(range(COPIES))

    def planned(src, dst, to):
        place = next(places)
        return pltpu.make_async_remote_copy(
            src_ref=src, dst_ref=dst, send_sem=ss.at[place], recv_sem=rs.at[place],
            device_id=to, device_id_type=MESH)

    def keep(src, dst, to):
        copy = planned(src, dst, to)
        copy.start()
        started.append(copy)
        return copy

    def same(ref, to):
        return keep(ref, ref, to)

    my_rows = pl.ds(core * 512, 512)
    loads = []
    for n, (src, dst) in enumerate((
        (l_ref, l_in), (dinv_ref.at[core], dinv_in), (lc_ref, lc_in),
        (bbar_ref.at[pl.ds(y * 256, 256)], b_in), (xbar_ref.at[my_rows], xbar_in), (x_ref, x_in),
    )):
        load = pltpu.make_async_copy(src, dst, ls.at[n])
        load.start()
        loads.append(load)

    barrier = pltpu.get_barrier_semaphore()
    partners = [at(dy=d) for d in (1, 2, 3)] + [at(dl=1), at(dcore=1), at(dl=1, dcore=1)]
    partners += [at(dh=j, dz=k) for j in range(2) for k in range(8) if j or k]
    for partner in partners:
        pl.semaphore_signal(barrier, inc=1, device_id=partner, device_id_type=MESH)

    loads[0].wait()
    for q in range(CHUNKS):
        for side in range(2):
            start = side * 512 + q * WIDE
            lg[q, h, z, side] = l_in[:, start : start + WIDE]
    loads[1].wait()
    loads[2].wait()
    gy[y, :, 0:512] = dinv_in[...]
    gy[y, :, 512:768] = jnp.where(core == 0, lc_in[:, 0:256], lc_in[:, 256:512])

    pl.semaphore_wait(barrier, len(partners))

    l_z, l_h, b_y, g_y, x_y = {}, {}, {}, {}, {}

    def l_first(q):
        mine = lg.at[q, h, z]
        for k in Z_ORDER:
            l_z[q, k] = same(mine, at(dz=k))
        l_h[q, 0] = same(mine, at(dh=1))

    l_first(0)
    for d in (2, 1, 3):
        rows = pl.ds((y + d) % 4 * 256, 256)
        b_y[d] = keep(bbar_ref.at[rows], bb.at[d - 1], at(dy=d))
    for d in (2, 1, 3):
        g_y[d] = same(gy.at[y], at(dy=d))
    for q in range(1, CHUNKS):
        l_first(q)
    for d in (1, 3, 2):
        x_y[d] = keep(x_ref.at[my_rows], xx.at[d - 1, core], at(dy=d))

    def take_b(d, value):
        cols = slice(d * 128, (d + 1) * 128)
        high, low = halves(value)
        bh[:, cols] = high
        bl[:, cols] = low
        high, low = halves(value.T)
        th[cols, :] = high
        tl[cols, :] = low

    loads[3].wait()
    take_b(0, b_in[...])
    loads[4].wait()
    xbt[...] = xbar_in[...].T
    loads[5].wait()
    high, low = halves(x_in[...])
    xh[:, 0:128] = high
    xl[:, 0:128] = low

    def l_forward(q):
        for k in Z_ORDER:
            l_z[q, k].wait_recv()
            l_h[q, k] = same(lg.at[q, h, (z + 8 - k) % 8], at(dh=1))

    l_forward(0)

    for d in (1, 3, 2):
        g_y[d].wait_recv()
    for part in range(4):
        start, width = STARTS[part], (part + 1) * 128
        gs[h, z, :, start : start + width] = gy[part, :, 0:width]
        gs[h, z, :, start + width : start + width + 256] = gy[part, :, 512:768]
    g_z = {k: same(gs.at[h, z], at(dz=k)) for k in Z_ORDER}
    g_h = {0: same(gs.at[h, z], at(dh=1))}

    for d in (1, 3, 2):
        b_y[d].wait_recv()
        take_b(d, bb[d - 1])
    r_c, r_y = {}, {}

    def corr_chunk(q):
        for k in (0,) + Z_ORDER:
            l_h[q, k].wait_recv()
        for side in range(2):
            high, low = halves(lg[q, :, :, side].reshape(256, WIDE))
            lh[q, side] = high
            ll[q, side] = low
        turned = (th[...], tl[...])
        csend[q] = dot3(turned, (lh[q, 1 - core], ll[q, 1 - core]), NN).reshape(4, 128, WIDE)
        r_c[q] = keep(csend.at[q], crv.at[q], at(dcore=1))
        cks[q] = dot3(turned, (lh[q, core], ll[q, core]), NN).reshape(4, 128, WIDE)

    def corr_out(q):
        r_c[q].wait_recv()
        for d in (2, 1, 3, 0):
            cks[q, d] += crv[q, d]
            if d:
                r_y[q, d] = keep(cks.at[q, d], yr.at[q, d - 1], at(dy=4 - d))

    for q in range(CHUNKS):
        if q + 1 < CHUNKS:
            l_forward(q + 1)
        corr_chunk(q)
        corr_out(q)

    x_c = {}
    for d in (1, 3, 2):
        x_y[d].wait_recv()
        x_c[d] = same(xx.at[d - 1, core], at(dcore=1))
    for d in (1, 3, 2):
        x_c[d].wait_recv()
        cols = slice(d * 128, (d + 1) * 128)
        high, low = halves(xx[d - 1].reshape(1024, 128))
        xh[:, cols] = high
        xl[:, cols] = low
    for part in range(4):
        rows = slice(part * 256, (part + 1) * 256)
        product = dot3((bh[...], bl[...]), (xh[rows, :], xl[rows, :]), NT)
        pp[:, :, :, rows] = product.reshape(2, 8, 16, 256)
    f_z = {k: keep(pp.at[:, (z + k) % 8], zr.at[k - 1], at(dz=k)) for k in Z_ORDER}

    r_l = {}

    def corr_last(q):
        for d in (1, 3, 2):
            r_y[q, d].wait_recv()
        accs[q] = (cks[q, 0] + yr[q, 0]) + (yr[q, 1] + yr[q, 2])
        r_l[q] = keep(accs.at[q], accr.at[q], at(dl=1))

    for q in range(CHUNKS - 1):
        corr_last(q)
    for k in Z_ORDER:
        g_z[k].wait_recv()
        g_h[k] = same(gs.at[h, (z + 8 - k) % 8], at(dh=1))
    corr_last(CHUNKS - 1)

    for k in (0,) + Z_ORDER:
        g_h[k].wait_recv()
    for part in range(4):
        start, width = STARTS[part], (part + 1) * 128
        rows = slice(part * 128, width)
        high, low = halves(gs[:, :, :, start : start + width].reshape(128, width))
        gh[rows, 0:width] = high
        gl[rows, 0:width] = low
        if width < 512:
            gh[rows, width:512] = jnp.zeros((128, 512 - width), BF16)
            gl[rows, width:512] = jnp.zeros((128, 512 - width), BF16)
        start += width
        high, low = halves(gs[:, :, :, start : start + 256].reshape(128, 256))
        gh[rows, 512:768] = high
        gl[rows, 512:768] = low
    for q in range(CHUNKS):
        r_l[q].wait_recv()

    def block_of(columns):
        return gh[:, columns], gl[:, columns]

    solve_cols, cross_cols = slice(0, 512), slice(512, 768)
    panel_copy = planned(pt, ot, at(dcore=1))
    cross_copy = planned(ch, ch, at(dcore=1))

    def corrected():
        return xbt[...] - jnp.concatenate([accs[q] + accr[q] for q in range(CHUNKS)], axis=1)

    @pl.when(core == 1)
    def _():
        late = dot3(halves(corrected()), block_of(solve_cols), NN)
        pt[...] = late
        panel_copy.start()
        ch[...] = dot3(halves(late), block_of(cross_cols), NN)
        cross_copy.start()

    @pl.when(core == 0)
    def _():
        rest = corrected()
        panel_copy.wait_recv()
        cross = dot3(halves(ot[...]), block_of(cross_cols), NN)
        cross_copy.wait_recv()
        rest = rest - jnp.concatenate([cross, ch[...]], axis=1)
        pt[...] = dot3(halves(rest), block_of(solve_cols), NN)
        panel_copy.start()

    def lanes(part):
        return pl.ds(pl.multiple_of(part * 128, 128), 128)

    t_y = {d: keep(pt.at[:, lanes((y + d) % 4)], ta.at[d - 1], at(dy=d)) for d in (2, 1, 3)}
    panels_ref[my_rows, :] = pt[...].T
    turned = [pt[:, lanes(y)].T]
    for d in (1, 2, 3):
        t_y[d].wait_recv()
        turned.append(ta[d - 1].T)
    rows = halves(jnp.concatenate(turned, axis=1))

    def x_rows(start):
        where = pl.ds(pl.multiple_of(start, 256), 256)
        return xh[where, :], xl[where, :]

    others = [(j, k) for k in (4, 3, 5, 2, 6, 1, 7, 0) for j in (1, 0) if j or k]

    def spread(cols):
        return [
            planned(ds.at[(h + j) % 2, (z + k) % 8, :, cols], er.at[j * 8 + k, :, cols], at(dh=j, dz=k))
            for j, k in others
        ]

    def total(cols):
        parts = [er[j * 8 + k, :, cols] for j, k in others]
        parts.append(ds[h, z, :, cols])
        while len(parts) > 1:
            parts = [a + b for a, b in zip(parts[::2], parts[1::2])] + parts[len(parts) // 2 * 2 :]
        return -parts[0]

    one, two = slice(0, 256), slice(256, 512)
    ds[:, :, :, one] = dot3(rows, x_rows(core * 512 + lo * 256), NT).reshape(2, 8, 8, 256)
    d_one, d_two = spread(one), spread(two)
    for copy in d_one:
        copy.start()
    started.extend(d_one)

    @pl.when(core == 1)
    def _():
        ds[:, :, :, two] = dot3(rows, x_rows(lo * 256), NT).reshape(2, 8, 8, 256)
        for copy in d_two:
            copy.start()

    for k in Z_ORDER:
        f_z[k].wait_recv()
    sums = pp[:, z]
    for k in range(7):
        sums = sums + zr[k]
    ps[...] = sums
    f_h = keep(ps.at[1 - h], hr, at(dh=1))

    @pl.when(core == 1)
    def _():
        for copy in d_two:
            copy.wait()
        fin[aux, :, two] = total(two)

    @pl.when(core == 0)
    def _():
        fin[aux, :, two] = jnp.zeros((8, 256), F32)

    for copy in d_one:
        copy.wait_recv()
    fin[aux, :, one] = total(one)
    d_a = [same(fin.at[aux], at(dl=j // 2, dcore=j % 2)) for j in (1, 2, 3)]

    panel_copy.wait_send()

    @pl.when(core == 1)
    def _():
        cross_copy.wait_send()
        panel_copy.wait_recv()

    panels_ref[pl.ds((1 - core) * 512, 512), :] = ot[...].T
    f_h.wait_recv()
    lbelow_ref[...] = -(ps[h] + hr[...])
    for copy in d_a:
        copy.wait_recv()
    for side in range(2):
        cols = slice(side * 256, (side + 1) * 256)
        for which in range(2):
            ldiag_ref[which, :, cols] = fin[side * 2 + which, :, one]
        lcross_ref[:, cols] = fin[side * 2 + 1, :, two]

    for copy in started:
        copy.wait_send()


def body(x_panels, xbar_panels, bbar_below, l_below, l_cross, dinv):
    def vmem(*shape, dtype=F32):
        return pltpu.VMEM(shape, dtype)

    outs = (
        jax.ShapeDtypeStruct((1024, 128), F32),
        jax.ShapeDtypeStruct((16, 1024), F32),
        jax.ShapeDtypeStruct((2, 8, 512), F32),
        jax.ShapeDtypeStruct((8, 512), F32),
    )
    scratch = [
        vmem(1024, 128), vmem(512, 128), vmem(256, 128),
        vmem(16, 1024), vmem(8, 512), vmem(8, 512),
        vmem(CHUNKS, 2, 8, 2, 16, WIDE),
        vmem(CHUNKS, 2, 256, WIDE, dtype=BF16), vmem(CHUNKS, 2, 256, WIDE, dtype=BF16),
        vmem(4, 8, 768), vmem(2, 8, 8, PACKED),
        vmem(512, 768, dtype=BF16), vmem(512, 768, dtype=BF16),
        vmem(3, 256, 128),
        vmem(256, 512, dtype=BF16), vmem(256, 512, dtype=BF16),
        vmem(512, 256, dtype=BF16), vmem(512, 256, dtype=BF16),
        vmem(3, 2, 512, 128),
        vmem(1024, 512, dtype=BF16), vmem(1024, 512, dtype=BF16),
        vmem(128, 512),
        vmem(CHUNKS, 4, 128, WIDE), vmem(CHUNKS, 4, 128, WIDE),
        vmem(CHUNKS, 4, 128, WIDE), vmem(CHUNKS, 3, 128, WIDE),
        vmem(CHUNKS, 128, WIDE), vmem(CHUNKS, 128, WIDE),
        vmem(128, 512), vmem(128, 512), vmem(128, 256), vmem(3, 128, 128),
        vmem(2, 8, 8, 512), vmem(16, 8, 512), vmem(4, 8, 512),
        vmem(2, 8, 16, 1024), vmem(7, 2, 16, 1024),
        vmem(2, 16, 1024), vmem(16, 1024),
        pltpu.SemaphoreType.DMA((COPIES,)), pltpu.SemaphoreType.DMA((COPIES,)),
        pltpu.SemaphoreType.DMA((LOADS,)),
    ]
    return pl.pallas_call(
        kernel,
        out_shape=outs,
        in_specs=[pl.BlockSpec(memory_space=pltpu.MemorySpace.HBM)] * 6,
        out_specs=(pl.BlockSpec(memory_space=pltpu.VMEM),) * 4,
        scratch_shapes=scratch,
        compiler_params=pltpu.CompilerParams(
            collective_id=0, has_side_effects=True, vmem_limit_bytes=60 * 1024 * 1024),
        name="panel_steps",
    )(x_panels, xbar_panels, bbar_below, l_below, l_cross, dinv)


def solution(mesh):
    in_specs = (
        P(None, "pair"),
        P(None, "pair"),
        P("aux", "pair"),
        P(("aux", "pair"), None),
        P("pair", None),
        P(None, "pair", None),
    )
    out_specs = (P(None, "pair"), P(("aux", "pair"), None), P(None, "pair", None), P("pair", None))
    return jax.shard_map(body, mesh=mesh, in_specs=in_specs, out_specs=out_specs, check_vma=False)
```

```python
import jax
import jax.numpy as jnp
from jax import lax
from jax.experimental import pallas as pl
from jax.experimental.pallas import tpu as pltpu
from jax.sharding import PartitionSpec as P

MESH = pl.DeviceIdType.MESH
F32 = jnp.float32
BF16 = jnp.bfloat16
NN = ((1,), (0,))
NT = ((1,), (1,))

CHUNKS = 4
WIDE = 512 // CHUNKS
COPIES = 200
LOADS = 6

G_START = 0
BELOW_AT = 3
G_TURNS = ((), (), (1, 7, 2), (6, 3, 5, 4))

Z_ORDER = (1, 7, 2, 6, 3, 5, 4)

STARTS = (0, 384, 896, 1536)
PACKED = 2304


def halves(value):
    high = value.astype(BF16)
    return high, (value - high.astype(F32)).astype(BF16)


def dot3(a, b, dims):
    def one(s, t):
        return lax.dot_general(s, t, (dims, ((), ())), preferred_element_type=F32)

    return one(a[0], b[0]) + (one(a[0], b[1]) + one(a[1], b[0]))


def kernel(
    x_ref, xbar_ref, bbar_ref, l_ref, lc_ref, dinv_ref,
    panels_ref, lbelow_ref, ldiag_ref, lcross_ref,
    x_in, xbar_in, b_in, l_in, lc_in, dinv_in,
    lg, lh, ll, gy, gs, gh, gl, bb, bh, bl, th, tl, xx, xh, xl, xbt,
    cks, csend, crv, yr, accs, accr, pt, ot, ch, ta,
    ds, er, fin, pp, pb, zr, ps, hr, hh, ph, zh,
    ss, rs, ls,
):
    pair = lax.axis_index("pair")
    aux = lax.axis_index("aux")
    y, h, z = pair // 16, (pair // 8) % 2, pair % 8
    lo, core = aux // 2, aux % 2

    def at(dy=0, dh=0, dz=0, dl=0, dcore=0):
        place = ((y + dy) % 4 * 2 + (h + dh) % 2) * 8 + (z + dz) % 8
        return (place, (lo + dl) % 2 * 2 + (core + dcore) % 2)

    started = []
    places = iter(range(COPIES))

    def planned(src, dst, to):
        place = next(places)
        return pltpu.make_async_remote_copy(
            src_ref=src, dst_ref=dst, send_sem=ss.at[place], recv_sem=rs.at[place],
            device_id=to, device_id_type=MESH)

    def keep(src, dst, to):
        copy = planned(src, dst, to)
        copy.start()
        started.append(copy)
        return copy

    def same(ref, to):
        return keep(ref, ref, to)

    my_rows = pl.ds(core * 512, 512)
    loads = []
    for n, (src, dst) in enumerate((
        (l_ref, l_in), (dinv_ref.at[core], dinv_in), (lc_ref, lc_in),
        (bbar_ref.at[pl.ds(y * 256, 256)], b_in), (xbar_ref.at[my_rows], xbar_in), (x_ref, x_in),
    )):
        load = pltpu.make_async_copy(src, dst, ls.at[n])
        load.start()
        loads.append(load)

    barrier = pltpu.get_barrier_semaphore()
    partners = [at(dy=d) for d in (1, 2, 3)] + [at(dl=1), at(dcore=1), at(dl=1, dcore=1)]
    partners += [at(dz=k) for k in range(1, 8)] + [at(dh=1)]
    for partner in partners:
        pl.semaphore_signal(barrier, inc=1, device_id=partner, device_id_type=MESH)

    loads[0].wait()
    for q in range(CHUNKS):
        for side in range(2):
            start = side * 512 + q * WIDE
            lg[q, h, z, side] = l_in[:, start : start + WIDE]
    loads[1].wait()
    loads[2].wait()
    gy[y, :, 0:512] = dinv_in[...]
    gy[y, :, 512:768] = jnp.where(core == 0, lc_in[:, 0:256], lc_in[:, 256:512])

    pl.semaphore_wait(barrier, len(partners))

    l_z, l_h, b_y, g_y, x_y = {}, {}, {}, {}, {}

    def l_first(q):
        mine = lg.at[q, h, z]
        for k in Z_ORDER:
            l_z[q, k] = same(mine, at(dz=k))
        l_h[q, 0] = same(mine, at(dh=1))

    l_first(0)
    for d in (2, 1, 3):
        rows = pl.ds((y + d) % 4 * 256, 256)
        b_y[d] = keep(bbar_ref.at[rows], bb.at[d - 1], at(dy=d))
    for d in (2, 1, 3):
        g_y[d] = same(gy.at[y], at(dy=d))
    for q in range(1, CHUNKS):
        l_first(q)
    for d in (1, 3, 2):
        x_y[d] = keep(x_ref.at[my_rows], xx.at[d - 1, core], at(dy=d))

    def take_b(d, value):
        cols = slice(d * 128, (d + 1) * 128)
        high, low = halves(value)
        bh[:, cols] = high
        bl[:, cols] = low
        high, low = halves(value.T)
        th[cols, :] = high
        tl[cols, :] = low

    loads[3].wait()
    take_b(0, b_in[...])
    loads[4].wait()
    xbt[...] = xbar_in[...].T
    loads[5].wait()
    high, low = halves(x_in[...])
    xh[:, 0:128] = high
    xl[:, 0:128] = low

    def l_forward(q):
        for k in Z_ORDER:
            l_z[q, k].wait_recv()
            l_h[q, k] = same(lg.at[q, h, (z + 8 - k) % 8], at(dh=1))

    l_forward(0)

    g_z, g_h = {}, {}

    def g_pack():
        for d in (1, 3, 2):
            g_y[d].wait_recv()
        for part in range(4):
            start, width = STARTS[part], (part + 1) * 128
            gs[h, z, :, start : start + width] = gy[part, :, 0:width]
            gs[h, z, :, start + width : start + width + 256] = gy[part, :, 512:768]

    def g_first():
        for k in Z_ORDER:
            g_z[k] = same(gs.at[h, z], at(dz=k))
        g_h[0] = same(gs.at[h, z], at(dh=1))

    def g_forward(some):
        for k in some:
            g_z[k].wait_recv()
            g_h[k] = same(gs.at[h, (z + 8 - k) % 8], at(dh=1))

    g_pack()

    for d in (1, 3, 2):
        b_y[d].wait_recv()
        take_b(d, bb[d - 1])
    r_c, r_y = {}, {}

    def corr_chunk(q):
        for k in (0,) + Z_ORDER:
            l_h[q, k].wait_recv()
        for side in range(2):
            high, low = halves(lg[q, :, :, side].reshape(256, WIDE))
            lh[q, side] = high
            ll[q, side] = low
        turned = (th[...], tl[...])
        csend[q] = dot3(turned, (lh[q, 1 - core], ll[q, 1 - core]), NN).reshape(4, 128, WIDE)
        r_c[q] = keep(csend.at[q], crv.at[q], at(dcore=1))
        cks[q] = dot3(turned, (lh[q, core], ll[q, core]), NN).reshape(4, 128, WIDE)

    def corr_out(q):
        r_c[q].wait_recv()
        for d in (2, 1, 3, 0):
            cks[q, d] += crv[q, d]
            if d:
                r_y[q, d] = keep(cks.at[q, d], yr.at[q, d - 1], at(dy=4 - d))

    x_c, f_z, f_h = {}, {}, {}

    def below_products():
        for d in (1, 3, 2):
            x_y[d].wait_recv()
            x_c[d] = same(xx.at[d - 1, core], at(dcore=1))
        for d in (1, 3, 2):
            x_c[d].wait_recv()
            cols = slice(d * 128, (d + 1) * 128)
            high, low = halves(xx[d - 1].reshape(1024, 128))
            xh[:, cols] = high
            xl[:, cols] = low
        for part in range(4):
            rows = slice(part * 256, (part + 1) * 256)
            product = dot3((bh[...], bl[...]), (xh[rows, :], xl[rows, :]), NT)
            product = product.reshape(2, 8, 16, 256)
            if part < 3:
                pp[:, :, :, rows] = product
            else:
                pb[...] = product
        for k in Z_ORDER:
            f_z[0, k] = keep(pp.at[:, (z + k) % 8], zr.at[k - 1], at(dz=k))

    def below_second():
        f_h[1].wait_recv()
        ph[...] = pb[h] + hh[...]
        for k in Z_ORDER:
            f_z[1, k] = keep(ph.at[(z + k) % 8], zh.at[k - 1], at(dz=k))

    for q in range(CHUNKS):
        if q + 1 < CHUNKS:
            l_forward(q + 1)
        if q == G_START:
            g_first()
        corr_chunk(q)
        corr_out(q)
        g_forward(G_TURNS[q])
        if q == BELOW_AT:
            below_products()

    r_l = {}

    def corr_last(q):
        for d in (1, 3, 2):
            r_y[q, d].wait_recv()
        accs[q] = (cks[q, 0] + yr[q, 0]) + (yr[q, 1] + yr[q, 2])
        r_l[q] = keep(accs.at[q], accr.at[q], at(dl=1))

    for q in range(CHUNKS):
        corr_last(q)

    for k in (0,) + Z_ORDER:
        g_h[k].wait_recv()
    for part in range(4):
        start, width = STARTS[part], (part + 1) * 128
        rows = slice(part * 128, width)
        high, low = halves(gs[:, :, :, start : start + width].reshape(128, width))
        gh[rows, 0:width] = high
        gl[rows, 0:width] = low
        if width < 512:
            gh[rows, width:512] = jnp.zeros((128, 512 - width), BF16)
            gl[rows, width:512] = jnp.zeros((128, 512 - width), BF16)
        start += width
        high, low = halves(gs[:, :, :, start : start + 256].reshape(128, 256))
        gh[rows, 512:768] = high
        gl[rows, 512:768] = low
    for q in range(CHUNKS):
        r_l[q].wait_recv()
    f_h[1] = keep(pb.at[1 - h], hh, at(dh=1))

    def block_of(columns):
        return gh[:, columns], gl[:, columns]

    solve_cols, cross_cols = slice(0, 512), slice(512, 768)
    panel_copy = planned(pt, ot, at(dcore=1))
    cross_copy = planned(ch, ch, at(dcore=1))

    def corrected():
        return xbt[...] - jnp.concatenate([accs[q] + accr[q] for q in range(CHUNKS)], axis=1)

    @pl.when(core == 1)
    def _():
        late = dot3(halves(corrected()), block_of(solve_cols), NN)
        pt[...] = late
        panel_copy.start()
        ch[...] = dot3(halves(late), block_of(cross_cols), NN)
        cross_copy.start()

    @pl.when(core == 0)
    def _():
        rest = corrected()
        panel_copy.wait_recv()
        cross = dot3(halves(ot[...]), block_of(cross_cols), NN)
        cross_copy.wait_recv()
        rest = rest - jnp.concatenate([cross, ch[...]], axis=1)
        pt[...] = dot3(halves(rest), block_of(solve_cols), NN)
        panel_copy.start()

    def lanes(part):
        return pl.ds(pl.multiple_of(part * 128, 128), 128)

    t_y = {d: keep(pt.at[:, lanes((y + d) % 4)], ta.at[d - 1], at(dy=d)) for d in (2, 1, 3)}
    panels_ref[my_rows, :] = pt[...].T
    turned = [pt[:, lanes(y)].T]
    for d in (1, 2, 3):
        t_y[d].wait_recv()
        turned.append(ta[d - 1].T)
    rows = halves(jnp.concatenate(turned, axis=1))

    def x_rows(start):
        where = pl.ds(pl.multiple_of(start, 256), 256)
        return xh[where, :], xl[where, :]

    others = [(j, k) for k in (4, 3, 5, 2, 6, 1, 7, 0) for j in (1, 0) if j or k]

    def spread(cols):
        return [
            planned(ds.at[(h + j) % 2, (z + k) % 8, :, cols], er.at[j * 8 + k, :, cols], at(dh=j, dz=k))
            for j, k in others
        ]

    def total(cols):
        parts = [er[j * 8 + k, :, cols] for j, k in others]
        parts.append(ds[h, z, :, cols])
        while len(parts) > 1:
            parts = [a + b for a, b in zip(parts[::2], parts[1::2])] + parts[len(parts) // 2 * 2 :]
        return -parts[0]

    one, two = slice(0, 256), slice(256, 512)
    ds[:, :, :, one] = dot3(rows, x_rows(core * 512 + lo * 256), NT).reshape(2, 8, 8, 256)
    d_one, d_two = spread(one), spread(two)
    for copy in d_one:
        copy.start()
    started.extend(d_one)

    @pl.when(core == 1)
    def _():
        ds[:, :, :, two] = dot3(rows, x_rows(lo * 256), NT).reshape(2, 8, 8, 256)
        for copy in d_two:
            copy.start()

    below_second()
    for k in Z_ORDER:
        f_z[0, k].wait_recv()
    sums = pp[:, z]
    for k in range(7):
        sums = sums + zr[k]
    ps[...] = sums
    f_h[0] = keep(ps.at[1 - h], hr, at(dh=1))

    @pl.when(core == 1)
    def _():
        for copy in d_two:
            copy.wait()
        fin[aux, :, two] = total(two)

    @pl.when(core == 0)
    def _():
        fin[aux, :, two] = jnp.zeros((8, 256), F32)

    for copy in d_one:
        copy.wait_recv()
    fin[aux, :, one] = total(one)
    d_a = [same(fin.at[aux], at(dl=j // 2, dcore=j % 2)) for j in (1, 2, 3)]

    panel_copy.wait_send()

    @pl.when(core == 1)
    def _():
        cross_copy.wait_send()
        panel_copy.wait_recv()

    panels_ref[pl.ds((1 - core) * 512, 512), :] = ot[...].T
    for k in Z_ORDER:
        f_z[1, k].wait_recv()
    sums = ph[z]
    for k in range(7):
        sums = sums + zh[k]
    lbelow_ref[:, 768:1024] = -sums
    f_h[0].wait_recv()
    lbelow_ref[:, 0:768] = -(ps[h] + hr[...])
    for copy in d_a:
        copy.wait_recv()
    for side in range(2):
        cols = slice(side * 256, (side + 1) * 256)
        for which in range(2):
            ldiag_ref[which, :, cols] = fin[side * 2 + which, :, one]
        lcross_ref[:, cols] = fin[side * 2 + 1, :, two]

    for copy in started:
        copy.wait_send()


def body(x_panels, xbar_panels, bbar_below, l_below, l_cross, dinv):
    def vmem(*shape, dtype=F32):
        return pltpu.VMEM(shape, dtype)

    outs = (
        jax.ShapeDtypeStruct((1024, 128), F32),
        jax.ShapeDtypeStruct((16, 1024), F32),
        jax.ShapeDtypeStruct((2, 8, 512), F32),
        jax.ShapeDtypeStruct((8, 512), F32),
    )
    scratch = [
        vmem(1024, 128), vmem(512, 128), vmem(256, 128),
        vmem(16, 1024), vmem(8, 512), vmem(8, 512),
        vmem(CHUNKS, 2, 8, 2, 16, WIDE),
        vmem(CHUNKS, 2, 256, WIDE, dtype=BF16), vmem(CHUNKS, 2, 256, WIDE, dtype=BF16),
        vmem(4, 8, 768), vmem(2, 8, 8, PACKED),
        vmem(512, 768, dtype=BF16), vmem(512, 768, dtype=BF16),
        vmem(3, 256, 128),
        vmem(256, 512, dtype=BF16), vmem(256, 512, dtype=BF16),
        vmem(512, 256, dtype=BF16), vmem(512, 256, dtype=BF16),
        vmem(3, 2, 512, 128),
        vmem(1024, 512, dtype=BF16), vmem(1024, 512, dtype=BF16),
        vmem(128, 512),
        vmem(CHUNKS, 4, 128, WIDE), vmem(CHUNKS, 4, 128, WIDE),
        vmem(CHUNKS, 4, 128, WIDE), vmem(CHUNKS, 3, 128, WIDE),
        vmem(CHUNKS, 128, WIDE), vmem(CHUNKS, 128, WIDE),
        vmem(128, 512), vmem(128, 512), vmem(128, 256), vmem(3, 128, 128),
        vmem(2, 8, 8, 512), vmem(16, 8, 512), vmem(4, 8, 512),
        vmem(2, 8, 16, 768), vmem(2, 8, 16, 256), vmem(7, 2, 16, 768),
        vmem(2, 16, 768), vmem(16, 768),
        vmem(8, 16, 256), vmem(8, 16, 256), vmem(7, 16, 256),
        pltpu.SemaphoreType.DMA((COPIES,)), pltpu.SemaphoreType.DMA((COPIES,)),
        pltpu.SemaphoreType.DMA((LOADS,)),
    ]
    return pl.pallas_call(
        kernel,
        out_shape=outs,
        in_specs=[pl.BlockSpec(memory_space=pltpu.MemorySpace.HBM)] * 6,
        out_specs=(pl.BlockSpec(memory_space=pltpu.VMEM),) * 4,
        scratch_shapes=scratch,
        compiler_params=pltpu.CompilerParams(
            collective_id=0, has_side_effects=True, vmem_limit_bytes=60 * 1024 * 1024),
        name="panel_steps",
    )(x_panels, xbar_panels, bbar_below, l_below, l_cross, dinv)


def solution(mesh):
    in_specs = (
        P(None, "pair"),
        P(None, "pair"),
        P("aux", "pair"),
        P(("aux", "pair"), None),
        P("pair", None),
        P(None, "pair", None),
    )
    out_specs = (P(None, "pair"), P(("aux", "pair"), None), P(None, "pair", None), P("pair", None))
    return jax.shard_map(body, mesh=mesh, in_specs=in_specs, out_specs=out_specs, check_vma=False)
```

```python
import jax
import jax.numpy as jnp
from jax import lax
from jax.experimental import pallas as pl
from jax.experimental.pallas import tpu as pltpu
from jax.sharding import PartitionSpec as P

MESH = pl.DeviceIdType.MESH
F32 = jnp.float32
BF16 = jnp.bfloat16
NN = ((1,), (0,))
NT = ((1,), (1,))

CHUNKS = 4
WIDE = 512 // CHUNKS
COPIES = 200
LOADS = 6

G_START = 0
BELOW_AT = 3
G_TURNS = ((), (), (1, 7, 2), (6, 3, 5, 4))

Z_ORDER = (1, 7, 2, 6, 3, 5, 4)

STARTS = (0, 384, 896, 1536)
PACKED = 2304


def halves(value):
    high = value.astype(BF16)
    return high, (value - high.astype(F32)).astype(BF16)


def dot3(a, b, dims):
    def one(s, t):
        return lax.dot_general(s, t, (dims, ((), ())), preferred_element_type=F32)

    return one(a[0], b[0]) + (one(a[0], b[1]) + one(a[1], b[0]))


def kernel(
    x_ref, xbar_ref, bbar_ref, l_ref, lc_ref, dinv_ref,
    panels_ref, lbelow_ref, ldiag_ref, lcross_ref,
    x_in, xbar_in, b_in, l_in, lc_in, dinv_in,
    lg, lh, ll, gy, gs, gh, gl, bb, bh, bl, th, tl, xx, xh, xl, xbt,
    cks, csend, crv, yr, accs, accr, pt, ot, ch, ta,
    ds, er, fin, pp, pb, zr, ps, hr, hh, ph, zh,
    ss, rs, ls,
):
    pair = lax.axis_index("pair")
    aux = lax.axis_index("aux")
    y, h, z = pair // 16, (pair // 8) % 2, pair % 8
    lo, core = aux // 2, aux % 2

    def at(dy=0, dh=0, dz=0, dl=0, dcore=0):
        place = ((y + dy) % 4 * 2 + (h + dh) % 2) * 8 + (z + dz) % 8
        return (place, (lo + dl) % 2 * 2 + (core + dcore) % 2)

    started = []
    places = iter(range(COPIES))

    def planned(src, dst, to):
        place = next(places)
        return pltpu.make_async_remote_copy(
            src_ref=src, dst_ref=dst, send_sem=ss.at[place], recv_sem=rs.at[place],
            device_id=to, device_id_type=MESH)

    def keep(src, dst, to):
        copy = planned(src, dst, to)
        copy.start()
        started.append(copy)
        return copy

    def same(ref, to):
        return keep(ref, ref, to)

    my_rows = pl.ds(core * 512, 512)
    loads = []
    for n, (src, dst) in enumerate((
        (l_ref, l_in), (dinv_ref.at[core], dinv_in), (lc_ref, lc_in),
        (bbar_ref.at[pl.ds(y * 256, 256)], b_in), (xbar_ref.at[my_rows], xbar_in), (x_ref, x_in),
    )):
        load = pltpu.make_async_copy(src, dst, ls.at[n])
        load.start()
        loads.append(load)

    barrier = pltpu.get_barrier_semaphore()
    partners = [at(dy=d) for d in (1, 2, 3)] + [at(dl=1), at(dcore=1), at(dl=1, dcore=1)]
    partners += [at(dz=k) for k in range(1, 8)] + [at(dh=1)]
    for partner in partners:
        pl.semaphore_signal(barrier, inc=1, device_id=partner, device_id_type=MESH)

    loads[0].wait()
    for q in range(CHUNKS):
        for side in range(2):
            start = side * 512 + q * WIDE
            lg[q, h, z, side] = l_in[:, start : start + WIDE]
    loads[1].wait()
    loads[2].wait()
    gy[y, :, 0:512] = dinv_in[...]
    gy[y, :, 512:768] = jnp.where(core == 0, lc_in[:, 0:256], lc_in[:, 256:512])

    pl.semaphore_wait(barrier, len(partners))

    l_z, l_h, b_y, g_y, x_y = {}, {}, {}, {}, {}

    def l_first(q):
        mine = lg.at[q, h, z]
        for k in Z_ORDER:
            l_z[q, k] = same(mine, at(dz=k))
        l_h[q, 0] = same(mine, at(dh=1))

    l_first(0)
    for d in (2, 1, 3):
        rows = pl.ds((y + d) % 4 * 256, 256)
        b_y[d] = keep(bbar_ref.at[rows], bb.at[d - 1], at(dy=d))
    for d in (2, 1, 3):
        g_y[d] = same(gy.at[y], at(dy=d))
    for q in range(1, CHUNKS):
        l_first(q)
    for d in (1, 3, 2):
        x_y[d] = keep(x_ref.at[my_rows], xx.at[d - 1, core], at(dy=d))

    def take_b(d, value):
        cols = slice(d * 128, (d + 1) * 128)
        high, low = halves(value)
        bh[:, cols] = high
        bl[:, cols] = low
        high, low = halves(value.T)
        th[cols, :] = high
        tl[cols, :] = low

    loads[3].wait()
    take_b(0, b_in[...])
    loads[4].wait()
    xbt[...] = xbar_in[...].T
    loads[5].wait()
    high, low = halves(x_in[...])
    xh[:, 0:128] = high
    xl[:, 0:128] = low

    def l_forward(q):
        for k in Z_ORDER:
            l_z[q, k].wait_recv()
            l_h[q, k] = same(lg.at[q, h, (z + 8 - k) % 8], at(dh=1))

    l_forward(0)

    g_z, g_h = {}, {}

    def g_pack():
        for d in (1, 3, 2):
            g_y[d].wait_recv()
        for part in range(4):
            start, width = STARTS[part], (part + 1) * 128
            gs[h, z, :, start : start + width] = gy[part, :, 0:width]
            gs[h, z, :, start + width : start + width + 256] = gy[part, :, 512:768]

    def g_first():
        for k in Z_ORDER:
            g_z[k] = same(gs.at[h, z], at(dz=k))
        g_h[0] = same(gs.at[h, z], at(dh=1))

    def g_forward(some):
        for k in some:
            g_z[k].wait_recv()
            g_h[k] = same(gs.at[h, (z + 8 - k) % 8], at(dh=1))

    g_pack()

    for d in (1, 3, 2):
        b_y[d].wait_recv()
        take_b(d, bb[d - 1])
    r_c, r_y = {}, {}

    def corr_chunk(q):
        for k in (0,) + Z_ORDER:
            l_h[q, k].wait_recv()
        for side in range(2):
            high, low = halves(lg[q, :, :, side].reshape(256, WIDE))
            lh[q, side] = high
            ll[q, side] = low
        turned = (th[...], tl[...])
        csend[q] = dot3(turned, (lh[q, 1 - core], ll[q, 1 - core]), NN).reshape(4, 128, WIDE)
        r_c[q] = keep(csend.at[q], crv.at[q], at(dcore=1))
        cks[q] = dot3(turned, (lh[q, core], ll[q, core]), NN).reshape(4, 128, WIDE)

    def corr_out(q):
        r_c[q].wait_recv()
        for d in (2, 1, 3, 0):
            cks[q, d] += crv[q, d]
            if d:
                r_y[q, d] = keep(cks.at[q, d], yr.at[q, d - 1], at(dy=4 - d))

    x_c, f_z, f_h = {}, {}, {}

    def below_products():
        for d in (1, 3, 2):
            x_y[d].wait_recv()
            x_c[d] = same(xx.at[d - 1, core], at(dcore=1))
        for d in (1, 3, 2):
            x_c[d].wait_recv()
            cols = slice(d * 128, (d + 1) * 128)
            high, low = halves(xx[d - 1].reshape(1024, 128))
            xh[:, cols] = high
            xl[:, cols] = low
        for part in range(4):
            rows = slice(part * 256, (part + 1) * 256)
            product = dot3((bh[...], bl[...]), (xh[rows, :], xl[rows, :]), NT)
            product = product.reshape(2, 8, 16, 256)
            if part < 2:
                pp[:, :, :, rows] = product
            else:
                pb[:, :, :, part % 2 * 256 : part % 2 * 256 + 256] = product
        for k in Z_ORDER:
            f_z[0, k] = keep(pp.at[:, (z + k) % 8], zr.at[k - 1], at(dz=k))

    def below_second():
        f_h[1].wait_recv()
        ph[...] = pb[h] + hh[...]
        for k in Z_ORDER:
            f_z[1, k] = keep(ph.at[(z + k) % 8], zh.at[k - 1], at(dz=k))

    for q in range(CHUNKS):
        if q + 1 < CHUNKS:
            l_forward(q + 1)
        if q == G_START:
            g_first()
        corr_chunk(q)
        corr_out(q)
        g_forward(G_TURNS[q])
        if q == BELOW_AT:
            below_products()

    r_l = {}

    def corr_last(q):
        for d in (1, 3, 2):
            r_y[q, d].wait_recv()
        accs[q] = (cks[q, 0] + yr[q, 0]) + (yr[q, 1] + yr[q, 2])
        r_l[q] = keep(accs.at[q], accr.at[q], at(dl=1))

    for q in range(CHUNKS):
        corr_last(q)

    for k in (0,) + Z_ORDER:
        g_h[k].wait_recv()
    for part in range(4):
        start, width = STARTS[part], (part + 1) * 128
        rows = slice(part * 128, width)
        high, low = halves(gs[:, :, :, start : start + width].reshape(128, width))
        gh[rows, 0:width] = high
        gl[rows, 0:width] = low
        if width < 512:
            gh[rows, width:512] = jnp.zeros((128, 512 - width), BF16)
            gl[rows, width:512] = jnp.zeros((128, 512 - width), BF16)
        start += width
        high, low = halves(gs[:, :, :, start : start + 256].reshape(128, 256))
        gh[rows, 512:768] = high
        gl[rows, 512:768] = low
    for q in range(CHUNKS):
        r_l[q].wait_recv()
    f_h[1] = keep(pb.at[1 - h], hh, at(dh=1))

    def block_of(columns):
        return gh[:, columns], gl[:, columns]

    solve_cols, cross_cols = slice(0, 512), slice(512, 768)
    panel_copy = planned(pt, ot, at(dcore=1))
    cross_copy = planned(ch, ch, at(dcore=1))

    def corrected():
        return xbt[...] - jnp.concatenate([accs[q] + accr[q] for q in range(CHUNKS)], axis=1)

    @pl.when(core == 1)
    def _():
        late = dot3(halves(corrected()), block_of(solve_cols), NN)
        pt[...] = late
        panel_copy.start()
        ch[...] = dot3(halves(late), block_of(cross_cols), NN)
        cross_copy.start()

    @pl.when(core == 0)
    def _():
        rest = corrected()
        panel_copy.wait_recv()
        cross = dot3(halves(ot[...]), block_of(cross_cols), NN)
        cross_copy.wait_recv()
        rest = rest - jnp.concatenate([cross, ch[...]], axis=1)
        pt[...] = dot3(halves(rest), block_of(solve_cols), NN)
        panel_copy.start()

    def lanes(part):
        return pl.ds(pl.multiple_of(part * 128, 128), 128)

    t_y = {d: keep(pt.at[:, lanes((y + d) % 4)], ta.at[d - 1], at(dy=d)) for d in (2, 1, 3)}
    panels_ref[my_rows, :] = pt[...].T
    turned = [pt[:, lanes(y)].T]
    for d in (1, 2, 3):
        t_y[d].wait_recv()
        turned.append(ta[d - 1].T)
    rows = halves(jnp.concatenate(turned, axis=1))

    def x_rows(start):
        where = pl.ds(pl.multiple_of(start, 256), 256)
        return xh[where, :], xl[where, :]

    others = [(j, k) for k in (4, 3, 5, 2, 6, 1, 7, 0) for j in (1, 0) if j or k]

    def spread(cols):
        return [
            planned(ds.at[(h + j) % 2, (z + k) % 8, :, cols], er.at[j * 8 + k, :, cols], at(dh=j, dz=k))
            for j, k in others
        ]

    def total(cols):
        parts = [er[j * 8 + k, :, cols] for j, k in others]
        parts.append(ds[h, z, :, cols])
        while len(parts) > 1:
            parts = [a + b for a, b in zip(parts[::2], parts[1::2])] + parts[len(parts) // 2 * 2 :]
        return -parts[0]

    one, two = slice(0, 256), slice(256, 512)
    ds[:, :, :, one] = dot3(rows, x_rows(core * 512 + lo * 256), NT).reshape(2, 8, 8, 256)
    d_one, d_two = spread(one), spread(two)
    for copy in d_one:
        copy.start()
    started.extend(d_one)

    @pl.when(core == 1)
    def _():
        ds[:, :, :, two] = dot3(rows, x_rows(lo * 256), NT).reshape(2, 8, 8, 256)
        for copy in d_two:
            copy.start()

    below_second()
    for k in Z_ORDER:
        f_z[0, k].wait_recv()
    sums = pp[:, z]
    for k in range(7):
        sums = sums + zr[k]
    ps[...] = sums
    f_h[0] = keep(ps.at[1 - h], hr, at(dh=1))

    @pl.when(core == 1)
    def _():
        for copy in d_two:
            copy.wait()
        fin[aux, :, two] = total(two)

    @pl.when(core == 0)
    def _():
        fin[aux, :, two] = jnp.zeros((8, 256), F32)

    for copy in d_one:
        copy.wait_recv()
    fin[aux, :, one] = total(one)
    d_a = [same(fin.at[aux], at(dl=j // 2, dcore=j % 2)) for j in (1, 2, 3)]

    panel_copy.wait_send()

    @pl.when(core == 1)
    def _():
        cross_copy.wait_send()
        panel_copy.wait_recv()

    panels_ref[pl.ds((1 - core) * 512, 512), :] = ot[...].T
    for k in Z_ORDER:
        f_z[1, k].wait_recv()
    sums = ph[z]
    for k in range(7):
        sums = sums + zh[k]
    lbelow_ref[:, 512:1024] = -sums
    f_h[0].wait_recv()
    lbelow_ref[:, 0:512] = -(ps[h] + hr[...])
    for copy in d_a:
        copy.wait_recv()
    for side in range(2):
        cols = slice(side * 256, (side + 1) * 256)
        for which in range(2):
            ldiag_ref[which, :, cols] = fin[side * 2 + which, :, one]
        lcross_ref[:, cols] = fin[side * 2 + 1, :, two]

    for copy in started:
        copy.wait_send()


def body(x_panels, xbar_panels, bbar_below, l_below, l_cross, dinv):
    def vmem(*shape, dtype=F32):
        return pltpu.VMEM(shape, dtype)

    outs = (
        jax.ShapeDtypeStruct((1024, 128), F32),
        jax.ShapeDtypeStruct((16, 1024), F32),
        jax.ShapeDtypeStruct((2, 8, 512), F32),
        jax.ShapeDtypeStruct((8, 512), F32),
    )
    scratch = [
        vmem(1024, 128), vmem(512, 128), vmem(256, 128),
        vmem(16, 1024), vmem(8, 512), vmem(8, 512),
        vmem(CHUNKS, 2, 8, 2, 16, WIDE),
        vmem(CHUNKS, 2, 256, WIDE, dtype=BF16), vmem(CHUNKS, 2, 256, WIDE, dtype=BF16),
        vmem(4, 8, 768), vmem(2, 8, 8, PACKED),
        vmem(512, 768, dtype=BF16), vmem(512, 768, dtype=BF16),
        vmem(3, 256, 128),
        vmem(256, 512, dtype=BF16), vmem(256, 512, dtype=BF16),
        vmem(512, 256, dtype=BF16), vmem(512, 256, dtype=BF16),
        vmem(3, 2, 512, 128),
        vmem(1024, 512, dtype=BF16), vmem(1024, 512, dtype=BF16),
        vmem(128, 512),
        vmem(CHUNKS, 4, 128, WIDE), vmem(CHUNKS, 4, 128, WIDE),
        vmem(CHUNKS, 4, 128, WIDE), vmem(CHUNKS, 3, 128, WIDE),
        vmem(CHUNKS, 128, WIDE), vmem(CHUNKS, 128, WIDE),
        vmem(128, 512), vmem(128, 512), vmem(128, 256), vmem(3, 128, 128),
        vmem(2, 8, 8, 512), vmem(16, 8, 512), vmem(4, 8, 512),
        vmem(2, 8, 16, 512), vmem(2, 8, 16, 512), vmem(7, 2, 16, 512),
        vmem(2, 16, 512), vmem(16, 512),
        vmem(8, 16, 512), vmem(8, 16, 512), vmem(7, 16, 512),
        pltpu.SemaphoreType.DMA((COPIES,)), pltpu.SemaphoreType.DMA((COPIES,)),
        pltpu.SemaphoreType.DMA((LOADS,)),
    ]
    return pl.pallas_call(
        kernel,
        out_shape=outs,
        in_specs=[pl.BlockSpec(memory_space=pltpu.MemorySpace.HBM)] * 6,
        out_specs=(pl.BlockSpec(memory_space=pltpu.VMEM),) * 4,
        scratch_shapes=scratch,
        compiler_params=pltpu.CompilerParams(
            collective_id=0, has_side_effects=True, vmem_limit_bytes=60 * 1024 * 1024),
        name="panel_steps",
    )(x_panels, xbar_panels, bbar_below, l_below, l_cross, dinv)


def solution(mesh):
    in_specs = (
        P(None, "pair"),
        P(None, "pair"),
        P("aux", "pair"),
        P(("aux", "pair"), None),
        P("pair", None),
        P(None, "pair", None),
    )
    out_specs = (P(None, "pair"), P(("aux", "pair"), None), P(None, "pair", None), P("pair", None))
    return jax.shard_map(body, mesh=mesh, in_specs=in_specs, out_specs=out_specs, check_vma=False)
```

```python
import jax
import jax.numpy as jnp
from jax import lax
from jax.experimental import pallas as pl
from jax.experimental.pallas import tpu as pltpu
from jax.sharding import PartitionSpec as P

MESH = pl.DeviceIdType.MESH
F32 = jnp.float32
BF16 = jnp.bfloat16
NN = ((1,), (0,))
NT = ((1,), (1,))

CHUNKS = 4
WIDE = 512 // CHUNKS
COPIES = 200
LOADS = 6

G_START = 0
BELOW_AT = 3
G_TURNS = ((), (), (1, 7, 2), (6, 3, 5, 4))

Z_ORDER = (1, 7, 2, 6, 3, 5, 4)

STARTS = (0, 384, 896, 1536)
PACKED = 2304


def halves(value):
    high = value.astype(BF16)
    return high, (value - high.astype(F32)).astype(BF16)


def dot3(a, b, dims):
    def one(s, t):
        return lax.dot_general(s, t, (dims, ((), ())), preferred_element_type=F32)

    return one(a[0], b[0]) + (one(a[0], b[1]) + one(a[1], b[0]))


def kernel(
    x_ref, xbar_ref, bbar_ref, l_ref, lc_ref, dinv_ref,
    panels_ref, lbelow_ref, ldiag_ref, lcross_ref,
    x_in, xbar_in, b_in, l_in, lc_in, dinv_in,
    lg, lh, ll, gy, gs, gh, gl, bb, bh, bl, th, tl, xx, xh, xl, xbt,
    cks, csend, crv, yr, accs, accr, pt, ot, ch, ta,
    ds, er, fin, pp, pb, zr, ps, hr, hh, ph, zh,
    ss, rs, ls,
):
    pair = lax.axis_index("pair")
    aux = lax.axis_index("aux")
    y, h, z = pair // 16, (pair // 8) % 2, pair % 8
    lo, core = aux // 2, aux % 2

    def at(dy=0, dh=0, dz=0, dl=0, dcore=0):
        place = ((y + dy) % 4 * 2 + (h + dh) % 2) * 8 + (z + dz) % 8
        return (place, (lo + dl) % 2 * 2 + (core + dcore) % 2)

    started = []
    places = iter(range(COPIES))

    def planned(src, dst, to):
        place = next(places)
        return pltpu.make_async_remote_copy(
            src_ref=src, dst_ref=dst, send_sem=ss.at[place], recv_sem=rs.at[place],
            device_id=to, device_id_type=MESH)

    def keep(src, dst, to):
        copy = planned(src, dst, to)
        copy.start()
        started.append(copy)
        return copy

    def same(ref, to):
        return keep(ref, ref, to)

    my_rows = pl.ds(core * 512, 512)
    loads = []
    for n, (src, dst) in enumerate((
        (l_ref, l_in), (dinv_ref.at[core], dinv_in), (lc_ref, lc_in),
        (bbar_ref.at[pl.ds(y * 256, 256)], b_in), (xbar_ref.at[my_rows], xbar_in), (x_ref, x_in),
    )):
        load = pltpu.make_async_copy(src, dst, ls.at[n])
        load.start()
        loads.append(load)

    barrier = pltpu.get_barrier_semaphore()
    partners = [at(dy=d) for d in (1, 2, 3)] + [at(dl=1), at(dcore=1)]
    partners += [at(dz=k) for k in range(1, 8)] + [at(dh=1)]
    for partner in partners:
        pl.semaphore_signal(barrier, inc=1, device_id=partner, device_id_type=MESH)

    loads[0].wait()
    for q in range(CHUNKS):
        for side in range(2):
            start = side * 512 + q * WIDE
            lg[q, h, z, side] = l_in[:, start : start + WIDE]
    loads[1].wait()
    loads[2].wait()
    gy[y, :, 0:512] = dinv_in[...]
    gy[y, :, 512:768] = jnp.where(core == 0, lc_in[:, 0:256], lc_in[:, 256:512])

    pl.semaphore_wait(barrier, len(partners))

    l_z, l_h, b_y, g_y, x_y = {}, {}, {}, {}, {}

    def l_first(q):
        mine = lg.at[q, h, z]
        for k in Z_ORDER:
            l_z[q, k] = same(mine, at(dz=k))
        l_h[q, 0] = same(mine, at(dh=1))

    l_first(0)
    for d in (2, 1, 3):
        rows = pl.ds((y + d) % 4 * 256, 256)
        b_y[d] = keep(bbar_ref.at[rows], bb.at[d - 1], at(dy=d))
    for d in (2, 1, 3):
        g_y[d] = same(gy.at[y], at(dy=d))
    for q in range(1, CHUNKS):
        l_first(q)
    for d in (1, 3, 2):
        x_y[d] = keep(x_ref.at[my_rows], xx.at[d - 1, core], at(dy=d))

    def take_b(d, value):
        cols = slice(d * 128, (d + 1) * 128)
        high, low = halves(value)
        bh[:, cols] = high
        bl[:, cols] = low
        high, low = halves(value.T)
        th[cols, :] = high
        tl[cols, :] = low

    loads[3].wait()
    take_b(0, b_in[...])
    loads[4].wait()
    xbt[...] = xbar_in[...].T
    loads[5].wait()
    high, low = halves(x_in[...])
    xh[:, 0:128] = high
    xl[:, 0:128] = low

    def l_forward(q):
        for k in Z_ORDER:
            l_z[q, k].wait_recv()
            l_h[q, k] = same(lg.at[q, h, (z + 8 - k) % 8], at(dh=1))

    l_forward(0)

    g_z, g_h = {}, {}

    def g_pack():
        for d in (1, 3, 2):
            g_y[d].wait_recv()
        for part in range(4):
            start, width = STARTS[part], (part + 1) * 128
            gs[h, z, :, start : start + width] = gy[part, :, 0:width]
            gs[h, z, :, start + width : start + width + 256] = gy[part, :, 512:768]

    def g_first():
        for k in Z_ORDER:
            g_z[k] = same(gs.at[h, z], at(dz=k))
        g_h[0] = same(gs.at[h, z], at(dh=1))

    def g_forward(some):
        for k in some:
            g_z[k].wait_recv()
            g_h[k] = same(gs.at[h, (z + 8 - k) % 8], at(dh=1))

    g_pack()

    for d in (1, 3, 2):
        b_y[d].wait_recv()
        take_b(d, bb[d - 1])
    r_c, r_y = {}, {}

    def corr_chunk(q):
        for k in (0,) + Z_ORDER:
            l_h[q, k].wait_recv()
        for side in range(2):
            high, low = halves(lg[q, :, :, side].reshape(256, WIDE))
            lh[q, side] = high
            ll[q, side] = low
        turned = (th[...], tl[...])
        csend[q] = dot3(turned, (lh[q, 1 - core], ll[q, 1 - core]), NN).reshape(4, 128, WIDE)
        r_c[q] = keep(csend.at[q], crv.at[q], at(dcore=1))
        cks[q] = dot3(turned, (lh[q, core], ll[q, core]), NN).reshape(4, 128, WIDE)

    def corr_out(q):
        r_c[q].wait_recv()
        for d in (2, 1, 3, 0):
            cks[q, d] += crv[q, d]
            if d:
                r_y[q, d] = keep(cks.at[q, d], yr.at[q, d - 1], at(dy=4 - d))

    x_c, f_z, f_h = {}, {}, {}

    def below_products():
        for d in (1, 3, 2):
            x_y[d].wait_recv()
            x_c[d] = same(xx.at[d - 1, core], at(dcore=1))
        for d in (1, 3, 2):
            x_c[d].wait_recv()
            cols = slice(d * 128, (d + 1) * 128)
            high, low = halves(xx[d - 1].reshape(1024, 128))
            xh[:, cols] = high
            xl[:, cols] = low
        for part in range(4):
            rows = slice(part * 256, (part + 1) * 256)
            product = dot3((bh[...], bl[...]), (xh[rows, :], xl[rows, :]), NT)
            product = product.reshape(2, 8, 16, 256)
            if part < 2:
                pp[:, :, :, rows] = product
            else:
                pb[:, :, :, part % 2 * 256 : part % 2 * 256 + 256] = product
        for k in Z_ORDER:
            f_z[0, k] = keep(pp.at[:, (z + k) % 8], zr.at[k - 1], at(dz=k))

    def below_second():
        f_h[1].wait_recv()
        ph[...] = pb[h] + hh[...]
        for k in Z_ORDER:
            f_z[1, k] = keep(ph.at[(z + k) % 8], zh.at[k - 1], at(dz=k))

    for q in range(CHUNKS):
        if q + 1 < CHUNKS:
            l_forward(q + 1)
        if q == G_START:
            g_first()
        corr_chunk(q)
        corr_out(q)
        g_forward(G_TURNS[q])
        if q == BELOW_AT:
            below_products()

    r_l = {}

    def corr_last(q):
        for d in (1, 3, 2):
            r_y[q, d].wait_recv()
        accs[q] = (cks[q, 0] + yr[q, 0]) + (yr[q, 1] + yr[q, 2])
        r_l[q] = keep(accs.at[q], accr.at[q], at(dl=1))

    for q in range(CHUNKS):
        corr_last(q)
    f_h[1] = keep(pb.at[1 - h], hh, at(dh=1))

    for k in (0,) + Z_ORDER:
        g_h[k].wait_recv()
    for part in range(4):
        start, width = STARTS[part], (part + 1) * 128
        rows = slice(part * 128, width)
        high, low = halves(gs[:, :, :, start : start + width].reshape(128, width))
        gh[rows, 0:width] = high
        gl[rows, 0:width] = low
        if width < 512:
            gh[rows, width:512] = jnp.zeros((128, 512 - width), BF16)
            gl[rows, width:512] = jnp.zeros((128, 512 - width), BF16)
        start += width
        high, low = halves(gs[:, :, :, start : start + 256].reshape(128, 256))
        gh[rows, 512:768] = high
        gl[rows, 512:768] = low
    for q in range(CHUNKS):
        r_l[q].wait_recv()

    def block_of(columns):
        return gh[:, columns], gl[:, columns]

    solve_cols, cross_cols = slice(0, 512), slice(512, 768)
    panel_copy = planned(pt, ot, at(dcore=1))
    cross_copy = planned(ch, ch, at(dcore=1))

    def corrected():
        return xbt[...] - jnp.concatenate([accs[q] + accr[q] for q in range(CHUNKS)], axis=1)

    @pl.when(core == 1)
    def _():
        late = dot3(halves(corrected()), block_of(solve_cols), NN)
        pt[...] = late
        panel_copy.start()
        ch[...] = dot3(halves(late), block_of(cross_cols), NN)
        cross_copy.start()

    @pl.when(core == 0)
    def _():
        rest = corrected()
        panel_copy.wait_recv()
        cross = dot3(halves(ot[...]), block_of(cross_cols), NN)
        cross_copy.wait_recv()
        rest = rest - jnp.concatenate([cross, ch[...]], axis=1)
        pt[...] = dot3(halves(rest), block_of(solve_cols), NN)
        panel_copy.start()

    def lanes(part):
        return pl.ds(pl.multiple_of(part * 128, 128), 128)

    t_y = {d: keep(pt.at[:, lanes((y + d) % 4)], ta.at[d - 1], at(dy=d)) for d in (2, 1, 3)}
    panels_ref[my_rows, :] = pt[...].T
    turned = [pt[:, lanes(y)].T]
    for d in (1, 2, 3):
        t_y[d].wait_recv()
        turned.append(ta[d - 1].T)
    rows = halves(jnp.concatenate(turned, axis=1))

    def x_rows(start):
        where = pl.ds(pl.multiple_of(start, 256), 256)
        return xh[where, :], xl[where, :]

    others = [(j, k) for k in (4, 3, 5, 2, 6, 1, 7, 0) for j in (1, 0) if j or k]

    def spread(cols):
        return [
            planned(ds.at[(h + j) % 2, (z + k) % 8, :, cols], er.at[j * 8 + k, :, cols], at(dh=j, dz=k))
            for j, k in others
        ]

    def total(cols):
        parts = [er[j * 8 + k, :, cols] for j, k in others]
        parts.append(ds[h, z, :, cols])
        while len(parts) > 1:
            parts = [a + b for a, b in zip(parts[::2], parts[1::2])] + parts[len(parts) // 2 * 2 :]
        return -parts[0]

    one, two = slice(0, 256), slice(256, 512)
    ds[:, :, :, one] = dot3(rows, x_rows(core * 512 + lo * 256), NT).reshape(2, 8, 8, 256)
    d_one, d_two = spread(one), spread(two)
    for copy in d_one:
        copy.start()
    started.extend(d_one)

    @pl.when(core == 1)
    def _():
        ds[:, :, :, two] = dot3(rows, x_rows(lo * 256), NT).reshape(2, 8, 8, 256)
        for copy in d_two:
            copy.start()

    below_second()
    for k in Z_ORDER:
        f_z[0, k].wait_recv()
    sums = pp[:, z]
    for k in range(7):
        sums = sums + zr[k]
    ps[...] = sums
    f_h[0] = keep(ps.at[1 - h], hr, at(dh=1))

    @pl.when(core == 1)
    def _():
        for copy in d_two:
            copy.wait()
        fin[aux, :, two] = total(two)

    @pl.when(core == 0)
    def _():
        fin[aux, :, two] = jnp.zeros((8, 256), F32)

    for copy in d_one:
        copy.wait_recv()
    fin[aux, :, one] = total(one)
    d_a = [same(fin.at[aux], at(dl=j // 2, dcore=j % 2)) for j in (1, 2, 3)]

    panel_copy.wait_send()

    @pl.when(core == 1)
    def _():
        cross_copy.wait_send()
        panel_copy.wait_recv()

    panels_ref[pl.ds((1 - core) * 512, 512), :] = ot[...].T
    for k in Z_ORDER:
        f_z[1, k].wait_recv()
    sums = ph[z]
    for k in range(7):
        sums = sums + zh[k]
    lbelow_ref[:, 512:1024] = -sums
    f_h[0].wait_recv()
    lbelow_ref[:, 0:512] = -(ps[h] + hr[...])
    for copy in d_a:
        copy.wait_recv()
    for side in range(2):
        cols = slice(side * 256, (side + 1) * 256)
        for which in range(2):
            ldiag_ref[which, :, cols] = fin[side * 2 + which, :, one]
        lcross_ref[:, cols] = fin[side * 2 + 1, :, two]

    for copy in started:
        copy.wait_send()


def body(x_panels, xbar_panels, bbar_below, l_below, l_cross, dinv):
    def vmem(*shape, dtype=F32):
        return pltpu.VMEM(shape, dtype)

    outs = (
        jax.ShapeDtypeStruct((1024, 128), F32),
        jax.ShapeDtypeStruct((16, 1024), F32),
        jax.ShapeDtypeStruct((2, 8, 512), F32),
        jax.ShapeDtypeStruct((8, 512), F32),
    )
    scratch = [
        vmem(1024, 128), vmem(512, 128), vmem(256, 128),
        vmem(16, 1024), vmem(8, 512), vmem(8, 512),
        vmem(CHUNKS, 2, 8, 2, 16, WIDE),
        vmem(CHUNKS, 2, 256, WIDE, dtype=BF16), vmem(CHUNKS, 2, 256, WIDE, dtype=BF16),
        vmem(4, 8, 768), vmem(2, 8, 8, PACKED),
        vmem(512, 768, dtype=BF16), vmem(512, 768, dtype=BF16),
        vmem(3, 256, 128),
        vmem(256, 512, dtype=BF16), vmem(256, 512, dtype=BF16),
        vmem(512, 256, dtype=BF16), vmem(512, 256, dtype=BF16),
        vmem(3, 2, 512, 128),
        vmem(1024, 512, dtype=BF16), vmem(1024, 512, dtype=BF16),
        vmem(128, 512),
        vmem(CHUNKS, 4, 128, WIDE), vmem(CHUNKS, 4, 128, WIDE),
        vmem(CHUNKS, 4, 128, WIDE), vmem(CHUNKS, 3, 128, WIDE),
        vmem(CHUNKS, 128, WIDE), vmem(CHUNKS, 128, WIDE),
        vmem(128, 512), vmem(128, 512), vmem(128, 256), vmem(3, 128, 128),
        vmem(2, 8, 8, 512), vmem(16, 8, 512), vmem(4, 8, 512),
        vmem(2, 8, 16, 512), vmem(2, 8, 16, 512), vmem(7, 2, 16, 512),
        vmem(2, 16, 512), vmem(16, 512),
        vmem(8, 16, 512), vmem(8, 16, 512), vmem(7, 16, 512),
        pltpu.SemaphoreType.DMA((COPIES,)), pltpu.SemaphoreType.DMA((COPIES,)),
        pltpu.SemaphoreType.DMA((LOADS,)),
    ]
    return pl.pallas_call(
        kernel,
        out_shape=outs,
        in_specs=[pl.BlockSpec(memory_space=pltpu.MemorySpace.HBM)] * 6,
        out_specs=(pl.BlockSpec(memory_space=pltpu.VMEM),) * 4,
        scratch_shapes=scratch,
        compiler_params=pltpu.CompilerParams(
            collective_id=0, has_side_effects=True, vmem_limit_bytes=60 * 1024 * 1024),
        name="panel_steps",
    )(x_panels, xbar_panels, bbar_below, l_below, l_cross, dinv)


def solution(mesh):
    in_specs = (
        P(None, "pair"),
        P(None, "pair"),
        P("aux", "pair"),
        P(("aux", "pair"), None),
        P("pair", None),
        P(None, "pair", None),
    )
    out_specs = (P(None, "pair"), P(("aux", "pair"), None), P(None, "pair", None), P("pair", None))
    return jax.shard_map(body, mesh=mesh, in_specs=in_specs, out_specs=out_specs, check_vma=False)
```
